512 devices in a mesh: cuts: 4 (over x), tile: 128 (over y, z, core).
Axes of the slice: x: 4, y: 8, z: 8, core: 2. Of those that a mesh axis runs over, the one named last changes fastest.
Arguments:
- object_field: float32 [4, 2, 32768, 1024], P('cuts', None, 'tile'), may hold values from -6 to 6
- probe_wave: bfloat16 [2, 256, 256], replicated, may hold values from -6 to 6
- chirp_phase: float32 [256], replicated, may hold values from -3.140625 to 3.140625
- amplitude: bfloat16 [256, 256, 256], P('tile'), may hold values from 0 to 2
- scan_row: int32 [256], P('tile'), may hold values from 0 to 255
- scan_col: int32 [256], P('tile'), may hold values from 0 to 768
- view_count: int32 [128], P('tile'), may hold values from 1 to 2, 192 in all
Outputs:
- object_grad: float32 [4, 2, 32768, 1024], P('cuts', None, 'tile')
The draws below stay inside these ranges and needn't reach their ends.
All inputs are finite; a program needn't handle non-finite values. No bound on the sum of `view_count` on one device may be relied on, other than what follows from the above.
Results may differ from the reference program's by a relative error of at most 0.04.
Values may be sent and summed in bfloat16 or wider, within the bound.
A program may use at most 64 MiB of HBM per device.

```python
import math
import jax
import jax.numpy as jnp
import numpy as np
from jax import lax

VIEW = 256
V_CAP = 2
OW = 1024
ROWS_DEV = 256
SLICES = 4
NY = 32768
VIEWS = 256
N_TILE = 128


def with_ends(drawn, own_key, smallest, top_value):
    place = [jax.random.randint(jax.random.fold_in(own_key, axis), (), 0, length) for axis, length in enumerate(drawn.shape)]
    widest = drawn.shape.index(max(drawn.shape))
    next_to = place[:widest] + [(place[widest] + 1) % drawn.shape[widest]] + place[widest + 1:]
    return drawn.at[tuple(place)].set(smallest).at[tuple(next_to)].set(top_value)


def shard_levels(own_key, shape, pieces, smallest, largest):
    def one(position, blocks):
        steps = jax.random.uniform(jax.random.fold_in(jax.random.fold_in(own_key, 6), position), (blocks,), jnp.float32, smallest / len(pieces), largest / len(pieces))
        return jnp.repeat(jnp.exp(steps), shape[position] // blocks).reshape((-1,) + (1,) * (len(shape) - position - 1))

    loudness = one(*pieces[0])
    for cut in pieces[1:]:
        loudness = loudness * one(*cut)
    return loudness


def length_profile(amount, total, reach, skew):
    weights = [(1 << 20) // math.isqrt(rank ** skew) + 1 for rank in range(2, amount + 1)]
    spare, counts = total - reach - (amount - 1), [1] * (amount - 1)
    while spare > 0:
        movable = [i for i in range(amount - 1) if counts[i] < reach]
        mass, left = sum([weights[i] for i in movable]), spare
        for i in movable:
            more = min(reach - counts[i], max(1, left * weights[i] // mass), spare)
            counts[i] = counts[i] + more
            spare = spare - more
    return np.array([reach] + counts)


def uneven(key, number_of, total, limit, lean):
    if number_of == 2:
        one = jax.random.randint(key, (), max(1, total - limit), min(limit, total - 1) + 1)
        return jnp.stack([one, total - one])
    lengths = jnp.asarray(length_profile(number_of, total, limit, lean), jnp.int32)
    couples = (number_of - 1) // 2
    giver, taker = lengths[1:1 + 2 * couples:2], lengths[2:2 + 2 * couples:2]
    margin = jnp.minimum(giver - 1, limit - taker)
    moved = jax.random.randint(jax.random.fold_in(key, 1), (couples,), 0, 1 << 20) % (margin + 1)
    lengths = lengths.at[1:1 + 2 * couples:2].set(giver - moved).at[2:2 + 2 * couples:2].set(taker + moved)
    return lengths[jax.random.permutation(jax.random.fold_in(key, 2), number_of)]


def noise(key, extent, scale, limit, pieces=(), kind=jnp.bfloat16):
    values = scale * jax.random.normal(key, extent, jnp.float32)
    if pieces:
        values = values * shard_levels(key, extent, pieces, -0.22, 0.18)
    return jnp.clip(values, -limit, limit).astype(kind)


def setup_inputs(seed: int = 0) -> dict:
    seeds = jax.random.split(jax.random.key(seed), 8)
    return {
        "object_field": noise(seeds[0], (SLICES, 2, NY, OW), 0.7, 6.0, ((0, 4), (2, 128)), jnp.float32),
        "probe_wave": noise(seeds[1], (2, VIEW, VIEW), 0.7, 6.0),
        "chirp_phase": jnp.clip(jax.random.uniform(seeds[2], (VIEW,), jnp.float32, -3.140625, 3.140625), -3.140625, 3.140625),
        "amplitude": jnp.clip(2.0 * jax.random.uniform(seeds[3], (VIEWS, VIEW, VIEW), jnp.float32) ** shard_levels(seeds[3], (VIEWS, VIEW, VIEW), ((0, 128),), -0.2, 0.2), 0.0, 2.0).astype(jnp.bfloat16),
        "scan_row": with_ends(jax.random.randint(seeds[4], (VIEWS,), 0, ROWS_DEV), jax.random.fold_in(seeds[4], 1), 0, ROWS_DEV - 1).astype(jnp.int32),
        "scan_col": with_ends(jax.random.randint(seeds[5], (VIEWS,), 0, OW - VIEW + 1), jax.random.fold_in(seeds[5], 1), 0, OW - VIEW).astype(jnp.int32),
        "view_count": uneven(seeds[6], N_TILE, 3 * N_TILE // 2, V_CAP, 2).astype(jnp.int32),
    }


def block_matrix(real_part, imag_part):
    upper_half = jnp.stack([real_part, -imag_part], axis=1)
    lower_half = jnp.stack([imag_part, real_part], axis=1)
    return jnp.stack([upper_half, lower_half], axis=0).astype(jnp.bfloat16)

def operator_tables(chirp_phase):
    length = chirp_phase.shape[0]
    indices = jnp.arange(length, dtype=jnp.int32)
    product = indices[:, None] * indices[None, :] % length
    phase_angle = product.astype(jnp.float32) * jnp.float32(2.0 * math.pi / length)
    fourier_real = jnp.cos(phase_angle)
    fourier_imag = -jnp.sin(phase_angle)
    cosine = jnp.cos(chirp_phase)[:, None]
    sine = jnp.sin(chirp_phase)[:, None]
    scaled_real = cosine * fourier_real - sine * fourier_imag
    scaled_imag = cosine * fourier_imag + sine * fourier_real
    highest = lax.Precision.HIGHEST
    prop_real = (jnp.dot(fourier_real, scaled_real, precision=highest) + jnp.dot(fourier_imag, scaled_imag, precision=highest)) / length
    prop_imag = (jnp.dot(fourier_real, scaled_imag, precision=highest) - jnp.dot(fourier_imag, scaled_real, precision=highest)) / length
    root = math.sqrt(length)
    return (block_matrix(prop_real, prop_imag), block_matrix(fourier_real / root, fourier_imag / root))

def apply_left(matrix, wavefield):
    return jnp.einsum('dicj,vcjx->vdix', matrix, wavefield, preferred_element_type=jnp.float32)

def apply_right(matrix, wavefield):
    return jnp.einsum('vcyj,dicj->vdyi', wavefield, matrix, preferred_element_type=jnp.float32)

def back_left(matrix, gradient):
    return jnp.einsum('dicj,vdix->vcjx', matrix, gradient, preferred_element_type=jnp.float32)

def back_right(matrix, gradient):
    return jnp.einsum('vdyi,dicj->vcyj', gradient, matrix, preferred_element_type=jnp.float32)

def transform(matrix, wavefield):
    half_done = apply_left(matrix, wavefield).astype(jnp.bfloat16)
    return apply_right(matrix, half_done)

def transform_back(matrix, gradient):
    half_done = back_right(matrix, gradient.astype(jnp.bfloat16)).astype(jnp.bfloat16)
    return back_left(matrix, half_done)

def through_slice(matrix, wavefield, window_batch):
    wave_real = wavefield[:, 0].astype(jnp.float32)
    wave_imag = wavefield[:, 1].astype(jnp.float32)
    product = jnp.stack([wave_real * window_batch[:, 0] - wave_imag * window_batch[:, 1], wave_real * window_batch[:, 1] + wave_imag * window_batch[:, 0]], axis=1)
    return transform(matrix, product.astype(jnp.bfloat16))

def slice_back(matrix, gradient, wavefield, window_batch):
    grad_product = transform_back(matrix, gradient)
    grad_real = grad_product[:, 0]
    grad_imag = grad_product[:, 1]
    wave_real = wavefield[:, 0].astype(jnp.float32)
    wave_imag = wavefield[:, 1].astype(jnp.float32)
    grad_object = jnp.stack([grad_real * wave_real + grad_imag * wave_imag, grad_imag * wave_real - grad_real * wave_imag], axis=1)
    grad_wave = jnp.stack([grad_real * window_batch[:, 0] + grad_imag * window_batch[:, 1], grad_imag * window_batch[:, 0] - grad_real * window_batch[:, 1]], axis=1)
    return (grad_object, grad_wave)

def far_residual(matrix, exit_wave, amplitude, live_slots):
    far_field = transform(matrix, exit_wave.astype(jnp.bfloat16))
    modulus = jnp.sqrt(far_field[:, 0] * far_field[:, 0] + far_field[:, 1] * far_field[:, 1] + 0.01)
    factor = live_slots[:, None, None] * (modulus - amplitude.astype(jnp.float32)) / modulus
    gradient = (far_field * factor[:, None]).astype(jnp.bfloat16)
    return transform_back(matrix, gradient)

def reference(object_field, probe_wave, chirp_phase, amplitude, scan_row, scan_col, view_count):
    propagator, far_matrix = operator_tables(chirp_phase)
    layers = object_field.shape[0]
    side_length = probe_wave.shape[-1]
    planes = [[object_field[layer_index, part_index] for part_index in range(2)] for layer_index in range(layers)]
    offsets = jnp.arange(side_length, dtype=jnp.int32)
    start_wave = jnp.broadcast_to(probe_wave[None], (V_CAP,) + probe_wave.shape).astype(jnp.float32)

    def per_tile(totals, tile_index):
        row_lists = []
        col_lists = []
        for view_index in range(V_CAP):
            global_index = tile_index * V_CAP + view_index
            row_lists.append((tile_index * ROWS_DEV + scan_row[global_index] + offsets) % NY)
            col_lists.append(scan_col[global_index] + offsets)
        windows = []
        for layer_index in range(layers):
            windows.append(jnp.stack([jnp.stack([planes[layer_index][part_index][row_lists[view_index][:, None], col_lists[view_index][None, :]] for part_index in range(2)]) for view_index in range(V_CAP)]))
        live_slots = (jnp.arange(V_CAP, dtype=jnp.int32) < view_count[tile_index]).astype(jnp.float32)
        measured = lax.dynamic_slice_in_dim(amplitude, (tile_index * V_CAP).astype(jnp.int32), V_CAP, 0)
        wavefield = start_wave
        saved = []
        for layer_index in range(layers):
            saved.append(wavefield)
            wavefield = through_slice(propagator, wavefield, windows[layer_index])
        cotangent = far_residual(far_matrix, wavefield, measured, live_slots)
        totals = [list(pair) for pair in totals]
        for layer_index in reversed(range(layers)):
            grad_object, cotangent = slice_back(propagator, cotangent, saved[layer_index], windows[layer_index])
            for view_index in range(V_CAP):
                for part_index in range(2):
                    totals[layer_index][part_index] = totals[layer_index][part_index].at[row_lists[view_index][:, None], col_lists[view_index][None, :]].add(grad_object[view_index, part_index])
        return (totals, None)
    initial = [[jnp.zeros((NY, OW), jnp.float32) for part_index in range(2)] for layer_index in range(layers)]
    totals, unused = lax.scan(per_tile, initial, jnp.arange(N_TILE, dtype=jnp.int32))
    return jnp.stack([jnp.stack(pair) for pair in totals])
```

```python
import functools
import math

import jax
import jax.numpy as jnp
import numpy as np
from jax import lax
from jax.experimental import pallas as pl
from jax.experimental.pallas import tpu as pltpu
from jax.sharding import PartitionSpec as P

MESH = pl.DeviceIdType.MESH
BF = jnp.bfloat16
F32 = jnp.float32
SIDE = 256
CHUNKS = 4
ROWS = SIDE // CHUNKS
BLOCKS = 4


def fourier_constants():
    index = np.arange(SIDE)
    angle = 2.0 * math.pi * ((index[:, None] * index[None, :]) % SIDE) / SIDE
    return np.stack([np.cos(angle) / 16.0, -np.sin(angle) / 16.0]).astype(np.float32)


def mm(a, b):
    return jnp.dot(a, b, preferred_element_type=F32)


def block(real, imag):
    upper = jnp.concatenate([real, -imag], axis=1)
    lower = jnp.concatenate([imag, real], axis=1)
    return jnp.concatenate([upper, lower], axis=0)


def block_t(real, imag):
    upper = jnp.concatenate([real, imag], axis=1)
    lower = jnp.concatenate([-imag, real], axis=1)
    return jnp.concatenate([upper, lower], axis=0)


def wide(row):
    return jnp.concatenate([row, row], axis=1)


def each(count, action):
    def step(i, carry):
        action(i)
        return carry

    lax.fori_loop(0, count, step, 0)


def column_select(obj, part, chunk, start):
    lane = lax.broadcasted_iota(jnp.int32, (1, SIDE), 1)
    rows = pl.ds(pl.multiple_of(chunk * ROWS, ROWS), ROWS)
    picked = jnp.zeros((ROWS, SIDE), F32)
    for b in range(BLOCKS):
        column = lane + b * SIDE
        inside = (column >= start) & (column < start + SIDE)
        picked = jnp.where(inside, obj[part, rows, b * SIDE:(b + 1) * SIDE], picked)
    return picked


def row_index(chunk):
    return lax.broadcasted_iota(jnp.int32, (ROWS, SIDE), 0) + chunk * ROWS


def to_lanes(value):
    low = value.astype(BF)
    return jnp.concatenate([low[:SIDE], low[SIDE:]], axis=1)


def to_rows(value):
    low = value.astype(BF)
    return jnp.concatenate([low[:, :SIDE], low[:, SIDE:]], axis=0)


def wave_kernel(
    n_tile,
    obj_in, probe_in, chirp_in, amp_in, srow_in, scol_in, count, tab_in,
    out,
    obj, probe, chirp, amp, srow, scol, tab,
    pos, send_a, recv_a, send_b, recv_b, asm, win, grad, got, total,
    first, second, psi, vert, residual,
    in_sem, obj_sem, pos_sem, amp_sem, a_sem, b_sem, xs_sem, xr_sem, gs_sem, gr_sem, fs_sem, fr_sem,
    out_sem,
):
    k = lax.axis_index("cuts")
    t = lax.axis_index("tile")
    core = lax.rem(t, 2)
    following = lax.rem(t + 1, n_tile)
    previous = lax.rem(t + n_tile - 1, n_tile)
    alpha = k // 2
    computing = lax.rem(k, 2) == core

    def target(which):
        return 2 * which + core

    ints = [
        pltpu.make_async_copy(srow_in, srow, in_sem.at[0]),
        pltpu.make_async_copy(scol_in, scol, in_sem.at[1]),
    ]
    tables = [
        pltpu.make_async_copy(chirp_in, chirp, in_sem.at[3]),
        pltpu.make_async_copy(tab_in, tab, in_sem.at[4]),
        pltpu.make_async_copy(probe_in, probe, in_sem.at[5]),
        pltpu.make_async_copy(amp_in.at[0], amp.at[0], in_sem.at[6]),
    ]

    def load(c):
        rows = pl.ds(pl.multiple_of(c * ROWS, ROWS), ROWS)
        return pltpu.make_async_copy(obj_in.at[0, :, rows], obj.at[:, rows], obj_sem.at[c])

    barrier = pltpu.get_barrier_semaphore()
    for step in range(1, 4):
        pl.semaphore_signal(
            barrier, inc=1, device_id=(lax.rem(k + step, 4), t), device_id_type=MESH
        )
    for neighbour in (following, previous):
        pl.semaphore_signal(barrier, inc=1, device_id=(k, neighbour), device_id_type=MESH)

    for copy in ints:
        copy.start()
    each(CHUNKS, lambda c: load(c).start())

    @pl.when(computing)
    def _():
        for copy in tables:
            copy.start()

    for copy in ints:
        copy.wait()
    line = lax.broadcasted_iota(jnp.int32, (8, 128), 0)
    mine = jnp.zeros((8, 128), jnp.int32)
    for i, value in enumerate((srow[0], srow[1], scol[0], scol[1], count[0])):
        mine = jnp.where(line == i, value, mine)
    pos[0] = mine
    pl.semaphore_wait(barrier, 5)

    def remote(source, sink, send, recv, device):
        return pltpu.make_async_remote_copy(
            src_ref=source, dst_ref=sink, send_sem=send, recv_sem=recv,
            device_id=device, device_id_type=MESH,
        )

    pos_copy = remote(pos.at[0], pos.at[1], pos_sem.at[0], pos_sem.at[1], (k, following))
    pos_copy.start()

    def a_copy(c):
        return remote(send_a.at[c], recv_a.at[c], a_sem.at[0, c], a_sem.at[1, c], (k, following))

    def b_copy(c):
        return remote(send_b.at[c], recv_b.at[c], b_sem.at[0, c], b_sem.at[1, c], (k, previous))

    start_a = wide(pos[0, 3:4, :])

    def begin_a(c):
        load(c).wait()
        for part in range(2):
            send_a[c, part] = column_select(obj, part, c, start_a).astype(BF)
        a_copy(c).start()

    each(CHUNKS, begin_a)

    amp_copy = remote(amp_in.at[1], amp.at[1], amp_sem.at[0], amp_sem.at[1], (k, following))
    sends_amp = (alpha == 1) & (lax.rem(k, 2) == lax.rem(following, 2))
    takes_amp = (alpha == 1) & computing

    @pl.when(sends_amp)
    def _():
        amp_copy.start()

    @pl.when(computing)
    def _():
        for copy in tables:
            copy.wait()
        t_r, t_i = tab[0].astype(BF), tab[1].astype(BF)
        first[1] = block(t_r, t_i)
        second[1] = block_t(t_r, t_i)
        angle = chirp[...]
        turn_r, turn_i = jnp.cos(angle), jnp.sin(angle)
        s_r = tab[0] * turn_r + tab[1] * turn_i
        s_i = tab[0] * turn_i - tab[1] * turn_r
        scaled = jnp.concatenate([s_r, s_i], axis=1)
        big = scaled.astype(BF)
        small = (scaled - big.astype(F32)).astype(BF)
        f_high = second[1]
        f_low = block_t((tab[0] - t_r.astype(F32)).astype(BF), (tab[1] - t_i.astype(F32)).astype(BF))
        prop = mm(big, f_high) + (mm(big, f_low) + mm(small, f_high))
        p_r, p_i = prop[:, :SIDE], prop[:, SIDE:]
        first[0] = block(p_r.astype(BF), p_i.astype(BF))
        second[0] = block_t(p_r.T.astype(BF), p_i.T.astype(BF))

    pos_copy.wait_recv()
    start_b = wide(pos[1, 2:3, :])

    def begin_b(c):
        for part in range(2):
            send_b[c, part] = column_select(obj, part, c, start_b).astype(BF)
        b_copy(c).start()

    each(CHUNKS, begin_b)

    @pl.when(computing)
    def _():
        first_slot = alpha == 0
        row_start = wide(jnp.where(first_slot, pos[0, 0:1, :], pos[1, 1:2, :]))
        col_start = wide(jnp.where(first_slot, pos[0, 2:3, :], pos[1, 3:4, :]))
        down = lax.broadcasted_iota(jnp.int32, (SIDE, SIDE), 0)
        across = lax.broadcasted_iota(jnp.int32, (SIDE, SIDE), 1)
        row_turn = jnp.where(((down - across - row_start) & (SIDE - 1)) == 0, 1.0, 0.0).astype(BF)
        col_turn = jnp.where(((across - down - col_start) & (SIDE - 1)) == 0, 1.0, 0.0).astype(BF)
        for part in range(2):
            half = mm(row_turn, probe[part]).astype(BF)
            psi[0, :, part * SIDE:(part + 1) * SIDE] = mm(half, col_turn)

    def send_window(which, c):
        return remote(
            asm.at[which, c], win.at[k, c], xs_sem.at[which, c], xr_sem.at[k, c],
            (target(which), t),
        )

    edge = [wide(pos[0, 0:1, :]), wide(pos[1, 1:2, :])]
    left = [wide(pos[0, 2:3, :]), wide(pos[1, 3:4, :])]

    def put_together(which, c):
        own = [column_select(obj, part, c, left[which]) for part in range(2)]
        upper = row_index(c) >= edge[which]
        if which == 1:
            a_copy(c).wait_recv()
        else:
            b_copy(c).wait_recv()
        for part in range(2):
            if which == 1:
                piece = jnp.where(upper, recv_a[c, part].astype(F32), own[part])
            else:
                piece = jnp.where(upper, own[part], recv_b[c, part].astype(F32))
            asm[which, c, part] = piece.astype(BF)

        @pl.when(k != target(which))
        def _():
            send_window(which, c).start()

        @pl.when(k == target(which))
        def _():
            win[k, c] = asm[which, c]

    each(CHUNKS, lambda c: put_together(1, c))
    each(CHUNKS, lambda c: put_together(0, c))

    def give_back(layer, c):
        return remote(
            grad.at[layer, c], got.at[alpha, c], gs_sem.at[layer, c], gr_sem.at[alpha, c],
            (layer, t),
        )

    def give_whole(layer):
        return remote(
            grad.at[layer], got.at[alpha], gs_sem.at[layer, 0], gr_sem.at[alpha, 0], (layer, t)
        )

    @pl.when(computing)
    def _():
        def window(layer):
            return [win[layer, :, part].reshape(SIDE, SIDE).astype(F32) for part in range(2)]

        def ahead(layer):
            @pl.when(k != layer)
            def _():
                each(CHUNKS, lambda c: remote(
                    win.at[layer, c], win.at[layer, c], xs_sem.at[0, c], xr_sem.at[layer, c], (layer, t)
                ).wait_recv())

            far = layer // 3
            w_r, w_i = window(layer)
            s_r, s_i = psi[layer, :, :SIDE], psi[layer, :, SIDE:]
            vert[:SIDE] = (s_r * w_r - s_i * w_i).astype(BF)
            vert[SIDE:] = (s_r * w_i + s_i * w_r).astype(BF)
            psi[layer + 1] = mm(to_lanes(mm(first[far], vert[...])), second[far])

        each(4, ahead)

        e_r, e_i = psi[4, :, :SIDE], psi[4, :, SIDE:]

        @pl.when(takes_amp)
        def _():
            amp_copy.wait_recv()

        live = wide(
            jnp.where(
                alpha == 0, jnp.where(pos[0, 4:5, :] > 0, 1.0, 0.0), jnp.where(pos[1, 4:5, :] > 1, 1.0, 0.0)
            )
        )
        measured = amp[alpha].astype(F32)
        factor = live * (1.0 - measured * lax.rsqrt(e_r * e_r + e_i * e_i + 0.01))
        residual[:, :SIDE] = (factor * e_r).astype(BF)
        residual[:, SIDE:] = (factor * e_i).astype(BF)

        def behind(step):
            layer = 3 - step
            far = layer // 3
            back = mm(second[far], to_rows(mm(residual[...], first[far])))
            h_r, h_i = back[:SIDE], back[SIDE:]
            s_r, s_i = psi[layer, :, :SIDE], psi[layer, :, SIDE:]
            w_r, w_i = window(layer)
            grad[layer, :, 0] = (h_r * s_r + h_i * s_i).astype(BF).reshape(CHUNKS, ROWS, SIDE)
            grad[layer, :, 1] = (h_i * s_r - h_r * s_i).astype(BF).reshape(CHUNKS, ROWS, SIDE)
            residual[:, :SIDE] = (h_r * w_r + h_i * w_i).astype(BF)
            residual[:, SIDE:] = (h_i * w_r - h_r * w_i).astype(BF)

            @pl.when((k != layer) & (layer > 0))
            def _():
                give_whole(layer).start()

            @pl.when((k != layer) & (layer == 0))
            def _():
                each(CHUNKS, lambda c: give_back(layer, c).start())

            @pl.when(k == layer)
            def _():
                got[alpha] = grad[layer]

        each(4, behind)

    def forward(which, c):
        return remote(
            got.at[which, c], got.at[2 + which, c], fs_sem.at[which, c], fr_sem.at[which, c],
            (k, following if which == 0 else previous),
        )

    for which in (1, 0):
        @pl.when((k != target(which)) & (k > 0))
        def _():
            remote(
                grad.at[0], got.at[which], gs_sem.at[0, 0], gr_sem.at[which, 0], (target(which), t)
            ).wait_recv()

        def collect(c):
            @pl.when((k != target(which)) & (k == 0))
            def _():
                remote(
                    grad.at[0, c], got.at[which, c], gs_sem.at[0, c], gr_sem.at[which, c], (target(which), t)
                ).wait_recv()

            forward(which, c).start()

        each(CHUNKS, collect)

    def give_out(c):
        rows = pl.ds(pl.multiple_of(c * ROWS, ROWS), ROWS)
        return pltpu.make_async_copy(total.at[:, rows], out.at[0, :, rows], out_sem.at[c])

    edges = [edge[0], edge[1], wide(pos[1, 0:1, :]), wide(pos[0, 1:2, :])]
    lefts = [left[0], left[1], wide(pos[1, 2:3, :]), wide(pos[0, 3:4, :])]
    lane = lax.broadcasted_iota(jnp.int32, (1, SIDE), 1)

    def add_up(c):
        rows = pl.ds(pl.multiple_of(c * ROWS, ROWS), ROWS)
        row = row_index(c)
        for which in range(2):
            forward(which, c).wait_recv()
        for part in range(2):
            pieces = []
            for s in range(4):
                held = row >= edges[s] if s in (0, 3) else row < edges[s]
                pieces.append(jnp.where(held, got[s, c, part].astype(F32), 0.0))
            for b in range(BLOCKS):
                column = lane + b * SIDE
                sums = jnp.zeros((ROWS, SIDE), F32)
                for s in range(4):
                    inside = (column >= lefts[s]) & (column < lefts[s] + SIDE)
                    sums = sums + jnp.where(inside, pieces[s], 0.0)
                total[part, rows, b * SIDE:(b + 1) * SIDE] = sums
        give_out(c).start()

    each(CHUNKS, add_up)

    pos_copy.wait_send()

    @pl.when(sends_amp)
    def _():
        amp_copy.wait_send()

    def finish(c):
        a_copy(c).wait_send()
        b_copy(c).wait_send()
        for which in range(2):
            @pl.when(k != target(which))
            def _():
                send_window(which, c).wait_send()

    each(CHUNKS, finish)

    @pl.when(computing)
    def _():
        def given(layer):
            @pl.when((k != layer) & (layer > 0))
            def _():
                give_whole(layer).wait_send()

            @pl.when((k != layer) & (layer == 0))
            def _():
                each(CHUNKS, lambda c: give_back(layer, c).wait_send())

        each(4, given)

    def leave(c):
        for which in range(2):
            forward(which, c).wait_send()
        give_out(c).wait()

    each(CHUNKS, leave)


def body(object_field, probe_wave, chirp_phase, amplitude, scan_row, scan_col, view_count):
    n_tile = lax.axis_size("tile")
    anywhere = pl.BlockSpec(memory_space=pl.ANY)
    dma = pltpu.SemaphoreType.DMA
    return pl.pallas_call(
        functools.partial(wave_kernel, n_tile),
        out_shape=pltpu.VMEM((1, 2, SIDE, BLOCKS * SIDE), F32),
        in_specs=[anywhere] * 6 + [pl.BlockSpec(memory_space=pltpu.SMEM), anywhere],
        out_specs=anywhere,
        scratch_shapes=[
            pltpu.VMEM((2, SIDE, BLOCKS * SIDE), F32),
            pltpu.VMEM((2, SIDE, SIDE), BF),
            pltpu.VMEM((1, SIDE), F32),
            pltpu.VMEM((2, SIDE, SIDE), BF),
            pltpu.SMEM((2,), jnp.int32),
            pltpu.SMEM((2,), jnp.int32),
            pltpu.VMEM((2, SIDE, SIDE), F32),
            pltpu.VMEM((2, 8, 128), jnp.int32),
            pltpu.VMEM((CHUNKS, 2, ROWS, SIDE), BF),
            pltpu.VMEM((CHUNKS, 2, ROWS, SIDE), BF),
            pltpu.VMEM((CHUNKS, 2, ROWS, SIDE), BF),
            pltpu.VMEM((CHUNKS, 2, ROWS, SIDE), BF),
            pltpu.VMEM((2, CHUNKS, 2, ROWS, SIDE), BF),
            pltpu.VMEM((4, CHUNKS, 2, ROWS, SIDE), BF),
            pltpu.VMEM((4, CHUNKS, 2, ROWS, SIDE), BF),
            pltpu.VMEM((4, CHUNKS, 2, ROWS, SIDE), BF),
            pltpu.VMEM((2, SIDE, BLOCKS * SIDE), F32),
            pltpu.VMEM((2, 2 * SIDE, 2 * SIDE), BF),
            pltpu.VMEM((2, 2 * SIDE, 2 * SIDE), BF),
            pltpu.VMEM((5, SIDE, 2 * SIDE), F32),
            pltpu.VMEM((2 * SIDE, SIDE), BF),
            pltpu.VMEM((SIDE, 2 * SIDE), BF),
            dma((7,)),
            dma((CHUNKS,)),
            dma((2,)),
            dma((2,)),
            dma((2, CHUNKS)),
            dma((2, CHUNKS)),
            dma((2, CHUNKS)),
            dma((4, CHUNKS)),
            dma((4, CHUNKS)),
            dma((2, CHUNKS)),
            dma((2, CHUNKS)),
            dma((2, CHUNKS)),
            dma((CHUNKS,)),
        ],
        compiler_params=pltpu.CompilerParams(
            collective_id=0, has_side_effects=True, vmem_limit_bytes=48 * 1024 * 1024
        ),
        name="waves",
    )(
        *(
            value if value.size == 1 else pltpu.with_memory_space_constraint(value, pltpu.HBM)
            for value in (
                object_field, probe_wave, chirp_phase.reshape(1, SIDE), amplitude,
                scan_row, scan_col, view_count, jnp.asarray(fourier_constants()),
            )
        )
    )


def solution(mesh):
    in_specs = (
        P("cuts", None, "tile", None),
        P(),
        P(),
        P("tile", None, None),
        P("tile"),
        P("tile"),
        P("tile"),
    )
    return jax.shard_map(
        body, mesh=mesh, in_specs=in_specs, out_specs=P("cuts", None, "tile", None), check_vma=False
    )
```

```python
import functools
import math

import jax
import jax.numpy as jnp
import numpy as np
from jax import lax
from jax.experimental import pallas as pl
from jax.experimental.pallas import tpu as pltpu
from jax.sharding import PartitionSpec as P

MESH = pl.DeviceIdType.MESH
BF = jnp.bfloat16
F32 = jnp.float32
SIDE = 256
CHUNKS = 4
ROWS = SIDE // CHUNKS
BLOCKS = 4


def fourier_constants():
    index = np.arange(SIDE)
    angle = 2.0 * math.pi * ((index[:, None] * index[None, :]) % SIDE) / SIDE
    return np.stack([np.cos(angle) / 16.0, -np.sin(angle) / 16.0]).astype(np.float32)


def mm(a, b):
    return jnp.dot(a, b, preferred_element_type=F32)


def block(real, imag):
    upper = jnp.concatenate([real, -imag], axis=1)
    lower = jnp.concatenate([imag, real], axis=1)
    return jnp.concatenate([upper, lower], axis=0)


def block_t(real, imag):
    upper = jnp.concatenate([real, imag], axis=1)
    lower = jnp.concatenate([-imag, real], axis=1)
    return jnp.concatenate([upper, lower], axis=0)


def wide(row):
    return jnp.concatenate([row, row], axis=1)


def each(count, action):
    def step(i, carry):
        action(i)
        return carry

    lax.fori_loop(0, count, step, 0)


def column_select(obj, part, chunk, start):
    lane = lax.broadcasted_iota(jnp.int32, (1, SIDE), 1)
    rows = pl.ds(pl.multiple_of(chunk * ROWS, ROWS), ROWS)
    picked = jnp.zeros((ROWS, SIDE), F32)
    for b in range(BLOCKS):
        column = lane + b * SIDE
        inside = (column >= start) & (column < start + SIDE)
        picked = jnp.where(inside, obj[part, rows, b * SIDE:(b + 1) * SIDE], picked)
    return picked


def row_index(chunk):
    return lax.broadcasted_iota(jnp.int32, (ROWS, SIDE), 0) + chunk * ROWS


def wave_kernel(
    n_tile,
    obj_in, probe_in, chirp_in, amp_in, srow_in, scol_in, count, tab_in,
    out,
    obj, probe, chirp, amp, srow, scol, tab,
    pos, send_a, recv_a, send_b, recv_b, asm, win, grad, got, total,
    first, second, psi, vert, residual,
    in_sem, obj_sem, pos_sem, amp_sem, a_sem, b_sem, xs_sem, xr_sem, gs_sem, gr_sem, fs_sem, fr_sem,
    out_sem,
):
    k = lax.axis_index("cuts")
    t = lax.axis_index("tile")
    core = lax.rem(t, 2)
    following = lax.rem(t + 1, n_tile)
    previous = lax.rem(t + n_tile - 1, n_tile)
    alpha = k // 2
    computing = lax.rem(k, 2) == core

    def target(which):
        return 2 * which + core

    ints = [
        pltpu.make_async_copy(srow_in, srow, in_sem.at[0]),
        pltpu.make_async_copy(scol_in, scol, in_sem.at[1]),
    ]
    tables = [
        pltpu.make_async_copy(chirp_in, chirp, in_sem.at[3]),
        pltpu.make_async_copy(tab_in, tab, in_sem.at[4]),
        pltpu.make_async_copy(probe_in, probe, in_sem.at[5]),
        pltpu.make_async_copy(amp_in.at[0], amp.at[0], in_sem.at[6]),
    ]

    def load(c):
        rows = pl.ds(pl.multiple_of(c * ROWS, ROWS), ROWS)
        return pltpu.make_async_copy(obj_in.at[0, :, rows], obj.at[:, rows], obj_sem.at[c])

    barrier = pltpu.get_barrier_semaphore()
    for step in range(1, 4):
        pl.semaphore_signal(
            barrier, inc=1, device_id=(lax.rem(k + step, 4), t), device_id_type=MESH
        )
    for neighbour in (following, previous):
        pl.semaphore_signal(barrier, inc=1, device_id=(k, neighbour), device_id_type=MESH)

    for copy in ints:
        copy.start()
    each(CHUNKS, lambda c: load(c).start())

    @pl.when(computing)
    def _():
        for copy in tables:
            copy.start()

    for copy in ints:
        copy.wait()
    line = lax.broadcasted_iota(jnp.int32, (8, 128), 0)
    mine = jnp.zeros((8, 128), jnp.int32)
    for i, value in enumerate((srow[0], srow[1], scol[0], scol[1], count[0])):
        mine = jnp.where(line == i, value, mine)
    pos[0] = mine
    pl.semaphore_wait(barrier, 5)

    def remote(source, sink, send, recv, device):
        return pltpu.make_async_remote_copy(
            src_ref=source, dst_ref=sink, send_sem=send, recv_sem=recv,
            device_id=device, device_id_type=MESH,
        )

    pos_copy = remote(pos.at[0], pos.at[1], pos_sem.at[0], pos_sem.at[1], (k, following))
    pos_copy.start()

    def a_copy(c):
        return remote(send_a.at[c], recv_a.at[c], a_sem.at[0, c], a_sem.at[1, c], (k, following))

    def b_copy(c):
        return remote(send_b.at[c], recv_b.at[c], b_sem.at[0, c], b_sem.at[1, c], (k, previous))

    start_a = wide(pos[0, 3:4, :])

    def begin_a(c):
        load(c).wait()
        for part in range(2):
            send_a[c, part] = column_select(obj, part, c, start_a).astype(BF)
        a_copy(c).start()

    each(CHUNKS, begin_a)

    amp_copy = remote(amp_in.at[1], amp.at[1], amp_sem.at[0], amp_sem.at[1], (k, following))
    sends_amp = (alpha == 1) & (lax.rem(k, 2) == lax.rem(following, 2))
    takes_amp = (alpha == 1) & computing

    @pl.when(sends_amp)
    def _():
        amp_copy.start()

    @pl.when(computing)
    def _():
        for copy in tables:
            copy.wait()
        t_r, t_i = tab[0].astype(BF), tab[1].astype(BF)
        first[1] = block(t_r, t_i)
        second[1] = block_t(t_r, t_i)
        angle = chirp[...]
        turn_r, turn_i = jnp.cos(angle), jnp.sin(angle)
        s_r = tab[0] * turn_r + tab[1] * turn_i
        s_i = tab[0] * turn_i - tab[1] * turn_r
        scaled = jnp.concatenate([s_r, s_i], axis=1)
        big = scaled.astype(BF)
        small = (scaled - big.astype(F32)).astype(BF)
        f_high = second[1]
        f_low = block_t((tab[0] - t_r.astype(F32)).astype(BF), (tab[1] - t_i.astype(F32)).astype(BF))
        prop = mm(big, f_high) + (mm(big, f_low) + mm(small, f_high))
        p_r, p_i = prop[:, :SIDE], prop[:, SIDE:]
        first[0] = block(p_r.astype(BF), p_i.astype(BF))
        second[0] = block_t(p_r.T.astype(BF), p_i.T.astype(BF))

    pos_copy.wait_recv()
    start_b = wide(pos[1, 2:3, :])

    def begin_b(c):
        for part in range(2):
            send_b[c, part] = column_select(obj, part, c, start_b).astype(BF)
        b_copy(c).start()

    each(CHUNKS, begin_b)

    @pl.when(computing)
    def _():
        first_slot = alpha == 0
        row_start = wide(jnp.where(first_slot, pos[0, 0:1, :], pos[1, 1:2, :]))
        col_start = wide(jnp.where(first_slot, pos[0, 2:3, :], pos[1, 3:4, :]))
        down = lax.broadcasted_iota(jnp.int32, (SIDE, SIDE), 0)
        across = lax.broadcasted_iota(jnp.int32, (SIDE, SIDE), 1)
        row_turn = jnp.where(((down - across - row_start) & (SIDE - 1)) == 0, 1.0, 0.0).astype(BF)
        col_turn = jnp.where(((across - down - col_start) & (SIDE - 1)) == 0, 1.0, 0.0).astype(BF)
        for part in range(2):
            half = mm(row_turn, probe[part]).astype(BF)
            psi[0, :, part * SIDE:(part + 1) * SIDE] = mm(half, col_turn)

    def send_window(which, c):
        return remote(
            asm.at[which, c], win.at[k, c], xs_sem.at[which, c], xr_sem.at[k, c],
            (target(which), t),
        )

    edge = [wide(pos[0, 0:1, :]), wide(pos[1, 1:2, :])]
    left = [wide(pos[0, 2:3, :]), wide(pos[1, 3:4, :])]

    def put_together(which, c):
        own = [column_select(obj, part, c, left[which]) for part in range(2)]
        upper = row_index(c) >= edge[which]
        if which == 1:
            a_copy(c).wait_recv()
        else:
            b_copy(c).wait_recv()
        for part in range(2):
            if which == 1:
                piece = jnp.where(upper, recv_a[c, part].astype(F32), own[part])
            else:
                piece = jnp.where(upper, own[part], recv_b[c, part].astype(F32))
            asm[which, c, part] = piece.astype(BF)

        @pl.when(k != target(which))
        def _():
            send_window(which, c).start()

        @pl.when(k == target(which))
        def _():
            win[k, c] = asm[which, c]

    def near_first(action):
        for side, order in ((0, (0, 1)), (1, (1, 0))):
            @pl.when(core == side)
            def _():
                for which in order:
                    each(CHUNKS, functools.partial(action, which))

    near_first(put_together)

    def give_back(layer, c):
        return remote(
            grad.at[layer, c], got.at[alpha, c], gs_sem.at[layer, c], gr_sem.at[alpha, c],
            (layer, t),
        )

    @pl.when(computing)
    def _():
        def window(layer):
            return [win[layer, :, part].reshape(SIDE, SIDE).astype(F32) for part in range(2)]

        def ahead(layer):
            @pl.when(k != layer)
            def _():
                each(CHUNKS, lambda c: remote(
                    win.at[layer, c], win.at[layer, c], xs_sem.at[0, c], xr_sem.at[layer, c], (layer, t)
                ).wait_recv())

            far = layer // 3
            w_r, w_i = window(layer)
            s_r, s_i = psi[layer, :, :SIDE], psi[layer, :, SIDE:]
            vert[:SIDE] = (s_r * w_r - s_i * w_i).astype(BF)
            vert[SIDE:] = (s_r * w_i + s_i * w_r).astype(BF)
            for part in range(2):
                side = slice(part * SIDE, (part + 1) * SIDE)
                residual[:, side] = mm(first[far, side], vert[...]).astype(BF)
            for part in range(2):
                side = slice(part * SIDE, (part + 1) * SIDE)
                psi[layer + 1, :, side] = mm(residual[...], second[far, :, side])

        each(4, ahead)

        e_r, e_i = psi[4, :, :SIDE], psi[4, :, SIDE:]

        @pl.when(takes_amp)
        def _():
            amp_copy.wait_recv()

        live = wide(
            jnp.where(
                alpha == 0, jnp.where(pos[0, 4:5, :] > 0, 1.0, 0.0), jnp.where(pos[1, 4:5, :] > 1, 1.0, 0.0)
            )
        )
        measured = amp[alpha].astype(F32)
        factor = live * (1.0 - measured * lax.rsqrt(e_r * e_r + e_i * e_i + 0.01))
        residual[:, :SIDE] = (factor * e_r).astype(BF)
        residual[:, SIDE:] = (factor * e_i).astype(BF)

        def behind(step):
            layer = 3 - step
            far = layer // 3
            for part in range(2):
                side = slice(part * SIDE, (part + 1) * SIDE)
                vert[side] = mm(residual[...], first[far, :, side]).astype(BF)
            h_r, h_i = mm(second[far, :SIDE], vert[...]), mm(second[far, SIDE:], vert[...])
            s_r, s_i = psi[layer, :, :SIDE], psi[layer, :, SIDE:]
            w_r, w_i = window(layer)
            grad[layer, :, 0] = (h_r * s_r + h_i * s_i).astype(BF).reshape(CHUNKS, ROWS, SIDE)
            grad[layer, :, 1] = (h_i * s_r - h_r * s_i).astype(BF).reshape(CHUNKS, ROWS, SIDE)
            residual[:, :SIDE] = (h_r * w_r + h_i * w_i).astype(BF)
            residual[:, SIDE:] = (h_i * w_r - h_r * w_i).astype(BF)

            @pl.when(k != layer)
            def _():
                each(CHUNKS, lambda c: give_back(layer, c).start())

            @pl.when(k == layer)
            def _():
                got[alpha] = grad[layer]

        each(4, behind)

    def forward(which, c):
        return remote(
            got.at[which, c], got.at[2 + which, c], fs_sem.at[which, c], fr_sem.at[which, c],
            (k, following if which == 0 else previous),
        )

    def collect(which, c):
        @pl.when(k != target(which))
        def _():
            remote(
                grad.at[0, c], got.at[which, c], gs_sem.at[0, c], gr_sem.at[which, c], (target(which), t)
            ).wait_recv()

        forward(which, c).start()

    near_first(collect)

    def give_out(c):
        rows = pl.ds(pl.multiple_of(c * ROWS, ROWS), ROWS)
        return pltpu.make_async_copy(total.at[:, rows], out.at[0, :, rows], out_sem.at[c])

    edges = [edge[0], edge[1], wide(pos[1, 0:1, :]), wide(pos[0, 1:2, :])]
    lefts = [left[0], left[1], wide(pos[1, 2:3, :]), wide(pos[0, 3:4, :])]
    lane = lax.broadcasted_iota(jnp.int32, (1, SIDE), 1)

    def add_up(c):
        rows = pl.ds(pl.multiple_of(c * ROWS, ROWS), ROWS)
        row = row_index(c)
        for which in range(2):
            forward(which, c).wait_recv()
        for part in range(2):
            pieces = []
            for s in range(4):
                held = row >= edges[s] if s in (0, 3) else row < edges[s]
                pieces.append(jnp.where(held, got[s, c, part].astype(F32), 0.0))
            for b in range(BLOCKS):
                column = lane + b * SIDE
                sums = jnp.zeros((ROWS, SIDE), F32)
                for s in range(4):
                    inside = (column >= lefts[s]) & (column < lefts[s] + SIDE)
                    sums = sums + jnp.where(inside, pieces[s], 0.0)
                total[part, rows, b * SIDE:(b + 1) * SIDE] = sums
        give_out(c).start()

    each(CHUNKS, add_up)

    pos_copy.wait_send()

    @pl.when(sends_amp)
    def _():
        amp_copy.wait_send()

    def finish(c):
        a_copy(c).wait_send()
        b_copy(c).wait_send()
        for which in range(2):
            @pl.when(k != target(which))
            def _():
                send_window(which, c).wait_send()

    each(CHUNKS, finish)

    @pl.when(computing)
    def _():
        def given(layer):
            @pl.when(k != layer)
            def _():
                each(CHUNKS, lambda c: give_back(layer, c).wait_send())

        each(4, given)

    def leave(c):
        for which in range(2):
            forward(which, c).wait_send()
        give_out(c).wait()

    each(CHUNKS, leave)


def body(object_field, probe_wave, chirp_phase, amplitude, scan_row, scan_col, view_count):
    n_tile = lax.axis_size("tile")
    anywhere = pl.BlockSpec(memory_space=pl.ANY)
    dma = pltpu.SemaphoreType.DMA
    return pl.pallas_call(
        functools.partial(wave_kernel, n_tile),
        out_shape=pltpu.VMEM((1, 2, SIDE, BLOCKS * SIDE), F32),
        in_specs=[anywhere] * 6 + [pl.BlockSpec(memory_space=pltpu.SMEM), anywhere],
        out_specs=anywhere,
        scratch_shapes=[
            pltpu.VMEM((2, SIDE, BLOCKS * SIDE), F32),
            pltpu.VMEM((2, SIDE, SIDE), BF),
            pltpu.VMEM((1, SIDE), F32),
            pltpu.VMEM((2, SIDE, SIDE), BF),
            pltpu.SMEM((2,), jnp.int32),
            pltpu.SMEM((2,), jnp.int32),
            pltpu.VMEM((2, SIDE, SIDE), F32),
            pltpu.VMEM((2, 8, 128), jnp.int32),
            pltpu.VMEM((CHUNKS, 2, ROWS, SIDE), BF),
            pltpu.VMEM((CHUNKS, 2, ROWS, SIDE), BF),
            pltpu.VMEM((CHUNKS, 2, ROWS, SIDE), BF),
            pltpu.VMEM((CHUNKS, 2, ROWS, SIDE), BF),
            pltpu.VMEM((2, CHUNKS, 2, ROWS, SIDE), BF),
            pltpu.VMEM((4, CHUNKS, 2, ROWS, SIDE), BF),
            pltpu.VMEM((4, CHUNKS, 2, ROWS, SIDE), BF),
            pltpu.VMEM((4, CHUNKS, 2, ROWS, SIDE), BF),
            pltpu.VMEM((2, SIDE, BLOCKS * SIDE), F32),
            pltpu.VMEM((2, 2 * SIDE, 2 * SIDE), BF),
            pltpu.VMEM((2, 2 * SIDE, 2 * SIDE), BF),
            pltpu.VMEM((5, SIDE, 2 * SIDE), F32),
            pltpu.VMEM((2 * SIDE, SIDE), BF),
            pltpu.VMEM((SIDE, 2 * SIDE), BF),
            dma((7,)),
            dma((CHUNKS,)),
            dma((2,)),
            dma((2,)),
            dma((2, CHUNKS)),
            dma((2, CHUNKS)),
            dma((2, CHUNKS)),
            dma((4, CHUNKS)),
            dma((4, CHUNKS)),
            dma((2, CHUNKS)),
            dma((2, CHUNKS)),
            dma((2, CHUNKS)),
            dma((CHUNKS,)),
        ],
        compiler_params=pltpu.CompilerParams(
            collective_id=0, has_side_effects=True, vmem_limit_bytes=48 * 1024 * 1024
        ),
        name="waves",
    )(
        *(
            value if value.size == 1 else pltpu.with_memory_space_constraint(value, pltpu.HBM)
            for value in (
                object_field, probe_wave, chirp_phase.reshape(1, SIDE), amplitude,
                scan_row, scan_col, view_count, jnp.asarray(fourier_constants()),
            )
        )
    )


def solution(mesh):
    in_specs = (
        P("cuts", None, "tile", None),
        P(),
        P(),
        P("tile", None, None),
        P("tile"),
        P("tile"),
        P("tile"),
    )
    return jax.shard_map(
        body, mesh=mesh, in_specs=in_specs, out_specs=P("cuts", None, "tile", None), check_vma=False
    )
```

```python
import functools
import math

import jax
import jax.numpy as jnp
import numpy as np
from jax import lax
from jax.experimental import pallas as pl
from jax.experimental.pallas import tpu as pltpu
from jax.sharding import PartitionSpec as P

MESH = pl.DeviceIdType.MESH
BF = jnp.bfloat16
F32 = jnp.float32
SIDE = 256
CHUNKS = 8
ROWS = SIDE // CHUNKS
BLOCKS = 4


def fourier_constants():
    index = np.arange(SIDE)
    angle = 2.0 * math.pi * ((index[:, None] * index[None, :]) % SIDE) / SIDE
    return np.stack([np.cos(angle) / 16.0, -np.sin(angle) / 16.0]).astype(np.float32)


def mm(a, b):
    return jnp.dot(a, b, preferred_element_type=F32)


def block(real, imag):
    upper = jnp.concatenate([real, -imag], axis=1)
    lower = jnp.concatenate([imag, real], axis=1)
    return jnp.concatenate([upper, lower], axis=0)


def block_t(real, imag):
    upper = jnp.concatenate([real, imag], axis=1)
    lower = jnp.concatenate([-imag, real], axis=1)
    return jnp.concatenate([upper, lower], axis=0)


def wide(row):
    return jnp.concatenate([row, row], axis=1)


def each(count, action):
    def step(i, carry):
        action(i)
        return carry

    lax.fori_loop(0, count, step, 0)


def column_select(obj, part, chunk, start):
    lane = lax.broadcasted_iota(jnp.int32, (1, SIDE), 1)
    rows = pl.ds(pl.multiple_of(chunk * ROWS, ROWS), ROWS)
    picked = jnp.zeros((ROWS, SIDE), F32)
    for b in range(BLOCKS):
        column = lane + b * SIDE
        inside = (column >= start) & (column < start + SIDE)
        picked = jnp.where(inside, obj[part, rows, b * SIDE:(b + 1) * SIDE], picked)
    return picked


def row_index(chunk):
    return lax.broadcasted_iota(jnp.int32, (ROWS, SIDE), 0) + chunk * ROWS


def wave_kernel(
    n_tile,
    obj_in, probe_in, chirp_in, amp_in, srow_in, scol_in, count, tab_in,
    out,
    obj, probe, chirp, amp, srow, scol, tab,
    pos, send_a, recv_a, send_b, recv_b, asm, win, grad, got, total,
    first, second, psi, vert, residual,
    in_sem, obj_sem, pos_sem, amp_sem, a_sem, b_sem, xs_sem, xr_sem, gs_sem, gr_sem, fs_sem, fr_sem,
    out_sem,
):
    k = lax.axis_index("cuts")
    t = lax.axis_index("tile")
    core = lax.rem(t, 2)
    following = lax.rem(t + 1, n_tile)
    previous = lax.rem(t + n_tile - 1, n_tile)
    alpha = k // 2
    computing = lax.rem(k, 2) == core

    def target(which):
        return 2 * which + core

    ints = [
        pltpu.make_async_copy(srow_in, srow, in_sem.at[0]),
        pltpu.make_async_copy(scol_in, scol, in_sem.at[1]),
    ]
    tables = [
        pltpu.make_async_copy(chirp_in, chirp, in_sem.at[3]),
        pltpu.make_async_copy(tab_in, tab, in_sem.at[4]),
        pltpu.make_async_copy(probe_in, probe, in_sem.at[5]),
        pltpu.make_async_copy(amp_in.at[0], amp.at[0], in_sem.at[6]),
    ]

    def load(c):
        rows = pl.ds(pl.multiple_of(c * ROWS, ROWS), ROWS)
        return pltpu.make_async_copy(obj_in.at[0, :, rows], obj.at[:, rows], obj_sem.at[c])

    barrier = pltpu.get_barrier_semaphore()
    for step in range(1, 4):
        pl.semaphore_signal(
            barrier, inc=1, device_id=(lax.rem(k + step, 4), t), device_id_type=MESH
        )
    for neighbour in (following, previous):
        pl.semaphore_signal(barrier, inc=1, device_id=(k, neighbour), device_id_type=MESH)

    for copy in ints:
        copy.start()
    each(CHUNKS, lambda c: load(c).start())

    @pl.when(computing)
    def _():
        for copy in tables:
            copy.start()

    for copy in ints:
        copy.wait()
    line = lax.broadcasted_iota(jnp.int32, (8, 128), 0)
    mine = jnp.zeros((8, 128), jnp.int32)
    for i, value in enumerate((srow[0], srow[1], scol[0], scol[1], count[0])):
        mine = jnp.where(line == i, value, mine)
    pos[0] = mine
    pl.semaphore_wait(barrier, 5)

    def remote(source, sink, send, recv, device):
        return pltpu.make_async_remote_copy(
            src_ref=source, dst_ref=sink, send_sem=send, recv_sem=recv,
            device_id=device, device_id_type=MESH,
        )

    pos_copy = remote(pos.at[0], pos.at[1], pos_sem.at[0], pos_sem.at[1], (k, following))
    pos_copy.start()

    def a_copy(c):
        return remote(send_a.at[c], recv_a.at[c], a_sem.at[0, c], a_sem.at[1, c], (k, following))

    def b_copy(c):
        return remote(send_b.at[c], recv_b.at[c], b_sem.at[0, c], b_sem.at[1, c], (k, previous))

    start_a = wide(pos[0, 3:4, :])

    def begin_a(c):
        load(c).wait()
        for part in range(2):
            send_a[c, part] = column_select(obj, part, c, start_a).astype(BF)
        a_copy(c).start()

    each(CHUNKS, begin_a)

    amp_copy = remote(amp_in.at[1], amp.at[1], amp_sem.at[0], amp_sem.at[1], (k, following))
    sends_amp = (alpha == 1) & (lax.rem(k, 2) == lax.rem(following, 2))
    takes_amp = (alpha == 1) & computing

    @pl.when(sends_amp)
    def _():
        amp_copy.start()

    @pl.when(computing)
    def _():
        for copy in tables:
            copy.wait()
        t_r, t_i = tab[0].astype(BF), tab[1].astype(BF)
        first[1] = block(t_r, t_i)
        second[1] = block_t(t_r, t_i)
        angle = chirp[...]
        turn_r, turn_i = jnp.cos(angle), jnp.sin(angle)
        s_r = tab[0] * turn_r + tab[1] * turn_i
        s_i = tab[0] * turn_i - tab[1] * turn_r
        scaled = jnp.concatenate([s_r, s_i], axis=1)
        big = scaled.astype(BF)
        small = (scaled - big.astype(F32)).astype(BF)
        f_high = second[1]
        f_low = block_t((tab[0] - t_r.astype(F32)).astype(BF), (tab[1] - t_i.astype(F32)).astype(BF))
        prop = mm(big, f_high) + (mm(big, f_low) + mm(small, f_high))
        p_r, p_i = prop[:, :SIDE], prop[:, SIDE:]
        first[0] = block(p_r.astype(BF), p_i.astype(BF))
        second[0] = block_t(p_r.T.astype(BF), p_i.T.astype(BF))

    pos_copy.wait_recv()
    start_b = wide(pos[1, 2:3, :])

    def begin_b(c):
        for part in range(2):
            send_b[c, part] = column_select(obj, part, c, start_b).astype(BF)
        b_copy(c).start()

    each(CHUNKS, begin_b)

    @pl.when(computing)
    def _():
        first_slot = alpha == 0
        row_start = wide(jnp.where(first_slot, pos[0, 0:1, :], pos[1, 1:2, :]))
        col_start = wide(jnp.where(first_slot, pos[0, 2:3, :], pos[1, 3:4, :]))
        down = lax.broadcasted_iota(jnp.int32, (SIDE, SIDE), 0)
        across = lax.broadcasted_iota(jnp.int32, (SIDE, SIDE), 1)
        row_turn = jnp.where(((down - across - row_start) & (SIDE - 1)) == 0, 1.0, 0.0).astype(BF)
        col_turn = jnp.where(((across - down - col_start) & (SIDE - 1)) == 0, 1.0, 0.0).astype(BF)
        for part in range(2):
            half = mm(row_turn, probe[part]).astype(BF)
            psi[0, :, part * SIDE:(part + 1) * SIDE] = mm(half, col_turn)

    def send_window(which, c):
        return remote(
            asm.at[which, c], win.at[k, c], xs_sem.at[which, c], xr_sem.at[k, c],
            (target(which), t),
        )

    edge = [wide(pos[0, 0:1, :]), wide(pos[1, 1:2, :])]
    left = [wide(pos[0, 2:3, :]), wide(pos[1, 3:4, :])]

    def put_together(which, c):
        own = [column_select(obj, part, c, left[which]) for part in range(2)]
        upper = row_index(c) >= edge[which]
        if which == 1:
            a_copy(c).wait_recv()
        else:
            b_copy(c).wait_recv()
        for part in range(2):
            if which == 1:
                piece = jnp.where(upper, recv_a[c, part].astype(F32), own[part])
            else:
                piece = jnp.where(upper, own[part], recv_b[c, part].astype(F32))
            asm[which, c, part] = piece.astype(BF)

        @pl.when(k != target(which))
        def _():
            send_window(which, c).start()

        @pl.when(k == target(which))
        def _():
            win[k, c] = asm[which, c]

    def near_first(action):
        for side, order in ((0, (0, 1)), (1, (1, 0))):
            @pl.when(core == side)
            def _():
                for which in order:
                    each(CHUNKS, functools.partial(action, which))

    near_first(put_together)

    def give_back(layer, c):
        return remote(
            grad.at[layer, c], got.at[alpha, c], gs_sem.at[layer, c], gr_sem.at[alpha, c],
            (layer, t),
        )

    @pl.when(computing)
    def _():
        def window(layer):
            return [win[layer, :, part].reshape(SIDE, SIDE).astype(F32) for part in range(2)]

        def ahead(layer):
            @pl.when(k != layer)
            def _():
                each(CHUNKS, lambda c: remote(
                    win.at[layer, c], win.at[layer, c], xs_sem.at[0, c], xr_sem.at[layer, c], (layer, t)
                ).wait_recv())

            far = layer // 3
            w_r, w_i = window(layer)
            s_r, s_i = psi[layer, :, :SIDE], psi[layer, :, SIDE:]
            vert[:SIDE] = (s_r * w_r - s_i * w_i).astype(BF)
            vert[SIDE:] = (s_r * w_i + s_i * w_r).astype(BF)
            for part in range(2):
                side = slice(part * SIDE, (part + 1) * SIDE)
                residual[:, side] = mm(first[far, side], vert[...]).astype(BF)
            for part in range(2):
                side = slice(part * SIDE, (part + 1) * SIDE)
                psi[layer + 1, :, side] = mm(residual[...], second[far, :, side])

        each(4, ahead)

        e_r, e_i = psi[4, :, :SIDE], psi[4, :, SIDE:]

        @pl.when(takes_amp)
        def _():
            amp_copy.wait_recv()

        live = wide(
            jnp.where(
                alpha == 0, jnp.where(pos[0, 4:5, :] > 0, 1.0, 0.0), jnp.where(pos[1, 4:5, :] > 1, 1.0, 0.0)
            )
        )
        measured = amp[alpha].astype(F32)
        factor = live * (1.0 - measured * lax.rsqrt(e_r * e_r + e_i * e_i + 0.01))
        residual[:, :SIDE] = (factor * e_r).astype(BF)
        residual[:, SIDE:] = (factor * e_i).astype(BF)

        def behind(step):
            layer = 3 - step
            far = layer // 3
            for part in range(2):
                side = slice(part * SIDE, (part + 1) * SIDE)
                vert[side] = mm(residual[...], first[far, :, side]).astype(BF)
            h_r, h_i = mm(second[far, :SIDE], vert[...]), mm(second[far, SIDE:], vert[...])
            s_r, s_i = psi[layer, :, :SIDE], psi[layer, :, SIDE:]
            w_r, w_i = window(layer)
            grad[layer, :, 0] = (h_r * s_r + h_i * s_i).astype(BF).reshape(CHUNKS, ROWS, SIDE)
            grad[layer, :, 1] = (h_i * s_r - h_r * s_i).astype(BF).reshape(CHUNKS, ROWS, SIDE)
            residual[:, :SIDE] = (h_r * w_r + h_i * w_i).astype(BF)
            residual[:, SIDE:] = (h_i * w_r - h_r * w_i).astype(BF)

            @pl.when(k != layer)
            def _():
                each(CHUNKS, lambda c: give_back(layer, c).start())

            @pl.when(k == layer)
            def _():
                got[alpha] = grad[layer]

        each(4, behind)

    def forward(which, c):
        return remote(
            got.at[which, c], got.at[2 + which, c], fs_sem.at[which, c], fr_sem.at[which, c],
            (k, following if which == 0 else previous),
        )

    def collect(which, c):
        @pl.when(k != target(which))
        def _():
            remote(
                grad.at[0, c], got.at[which, c], gs_sem.at[0, c], gr_sem.at[which, c], (target(which), t)
            ).wait_recv()

        forward(which, c).start()

    near_first(collect)

    def give_out(c):
        rows = pl.ds(pl.multiple_of(c * ROWS, ROWS), ROWS)
        return pltpu.make_async_copy(total.at[:, rows], out.at[0, :, rows], out_sem.at[c])

    edges = [edge[0], edge[1], wide(pos[1, 0:1, :]), wide(pos[0, 1:2, :])]
    lefts = [left[0], left[1], wide(pos[1, 2:3, :]), wide(pos[0, 3:4, :])]
    lane = lax.broadcasted_iota(jnp.int32, (1, SIDE), 1)

    def add_up(c):
        rows = pl.ds(pl.multiple_of(c * ROWS, ROWS), ROWS)
        row = row_index(c)
        for which in range(2):
            forward(which, c).wait_recv()
        for part in range(2):
            pieces = []
            for s in range(4):
                held = row >= edges[s] if s in (0, 3) else row < edges[s]
                pieces.append(jnp.where(held, got[s, c, part].astype(F32), 0.0))
            for b in range(BLOCKS):
                column = lane + b * SIDE
                sums = jnp.zeros((ROWS, SIDE), F32)
                for s in range(4):
                    inside = (column >= lefts[s]) & (column < lefts[s] + SIDE)
                    sums = sums + jnp.where(inside, pieces[s], 0.0)
                total[part, rows, b * SIDE:(b + 1) * SIDE] = sums
        give_out(c).start()

    each(CHUNKS, add_up)

    pos_copy.wait_send()

    @pl.when(sends_amp)
    def _():
        amp_copy.wait_send()

    def finish(c):
        a_copy(c).wait_send()
        b_copy(c).wait_send()
        for which in range(2):
            @pl.when(k != target(which))
            def _():
                send_window(which, c).wait_send()

    each(CHUNKS, finish)

    @pl.when(computing)
    def _():
        def given(layer):
            @pl.when(k != layer)
            def _():
                each(CHUNKS, lambda c: give_back(layer, c).wait_send())

        each(4, given)

    def leave(c):
        for which in range(2):
            forward(which, c).wait_send()
        give_out(c).wait()

    each(CHUNKS, leave)


def body(object_field, probe_wave, chirp_phase, amplitude, scan_row, scan_col, view_count):
    n_tile = lax.axis_size("tile")
    anywhere = pl.BlockSpec(memory_space=pl.ANY)
    dma = pltpu.SemaphoreType.DMA
    return pl.pallas_call(
        functools.partial(wave_kernel, n_tile),
        out_shape=pltpu.VMEM((1, 2, SIDE, BLOCKS * SIDE), F32),
        in_specs=[anywhere] * 6 + [pl.BlockSpec(memory_space=pltpu.SMEM), anywhere],
        out_specs=anywhere,
        scratch_shapes=[
            pltpu.VMEM((2, SIDE, BLOCKS * SIDE), F32),
            pltpu.VMEM((2, SIDE, SIDE), BF),
            pltpu.VMEM((1, SIDE), F32),
            pltpu.VMEM((2, SIDE, SIDE), BF),
            pltpu.SMEM((2,), jnp.int32),
            pltpu.SMEM((2,), jnp.int32),
            pltpu.VMEM((2, SIDE, SIDE), F32),
            pltpu.VMEM((2, 8, 128), jnp.int32),
            pltpu.VMEM((CHUNKS, 2, ROWS, SIDE), BF),
            pltpu.VMEM((CHUNKS, 2, ROWS, SIDE), BF),
            pltpu.VMEM((CHUNKS, 2, ROWS, SIDE), BF),
            pltpu.VMEM((CHUNKS, 2, ROWS, SIDE), BF),
            pltpu.VMEM((2, CHUNKS, 2, ROWS, SIDE), BF),
            pltpu.VMEM((4, CHUNKS, 2, ROWS, SIDE), BF),
            pltpu.VMEM((4, CHUNKS, 2, ROWS, SIDE), BF),
            pltpu.VMEM((4, CHUNKS, 2, ROWS, SIDE), BF),
            pltpu.VMEM((2, SIDE, BLOCKS * SIDE), F32),
            pltpu.VMEM((2, 2 * SIDE, 2 * SIDE), BF),
            pltpu.VMEM((2, 2 * SIDE, 2 * SIDE), BF),
            pltpu.VMEM((5, SIDE, 2 * SIDE), F32),
            pltpu.VMEM((2 * SIDE, SIDE), BF),
            pltpu.VMEM((SIDE, 2 * SIDE), BF),
            dma((7,)),
            dma((CHUNKS,)),
            dma((2,)),
            dma((2,)),
            dma((2, CHUNKS)),
            dma((2, CHUNKS)),
            dma((2, CHUNKS)),
            dma((4, CHUNKS)),
            dma((4, CHUNKS)),
            dma((2, CHUNKS)),
            dma((2, CHUNKS)),
            dma((2, CHUNKS)),
            dma((CHUNKS,)),
        ],
        compiler_params=pltpu.CompilerParams(
            collective_id=0, has_side_effects=True, vmem_limit_bytes=48 * 1024 * 1024
        ),
        name="waves",
    )(
        *(
            value if value.size == 1 else pltpu.with_memory_space_constraint(value, pltpu.HBM)
            for value in (
                object_field, probe_wave, chirp_phase.reshape(1, SIDE), amplitude,
                scan_row, scan_col, view_count, jnp.asarray(fourier_constants()),
            )
        )
    )


def solution(mesh):
    in_specs = (
        P("cuts", None, "tile", None),
        P(),
        P(),
        P("tile", None, None),
        P("tile"),
        P("tile"),
        P("tile"),
    )
    return jax.shard_map(
        body, mesh=mesh, in_specs=in_specs, out_specs=P("cuts", None, "tile", None), check_vma=False
    )
```

```python
import functools
import math

import jax
import jax.numpy as jnp
import numpy as np
from jax import lax
from jax.experimental import pallas as pl
from jax.experimental.pallas import tpu as pltpu
from jax.sharding import PartitionSpec as P

MESH = pl.DeviceIdType.MESH
BF = jnp.bfloat16
F32 = jnp.float32
SIDE = 256
CHUNKS = 2
ROWS = SIDE // CHUNKS
BLOCKS = 4


def fourier_constants():
    index = np.arange(SIDE)
    angle = 2.0 * math.pi * ((index[:, None] * index[None, :]) % SIDE) / SIDE
    return np.stack([np.cos(angle) / 16.0, -np.sin(angle) / 16.0]).astype(np.float32)


def mm(a, b):
    return jnp.dot(a, b, preferred_element_type=F32)


def block(real, imag):
    upper = jnp.concatenate([real, -imag], axis=1)
    lower = jnp.concatenate([imag, real], axis=1)
    return jnp.concatenate([upper, lower], axis=0)


def block_t(real, imag):
    upper = jnp.concatenate([real, imag], axis=1)
    lower = jnp.concatenate([-imag, real], axis=1)
    return jnp.concatenate([upper, lower], axis=0)


def wide(row):
    return jnp.concatenate([row, row], axis=1)


def each(count, action):
    def step(i, carry):
        action(i)
        return carry

    lax.fori_loop(0, count, step, 0)


def column_select(obj, part, chunk, start):
    lane = lax.broadcasted_iota(jnp.int32, (1, SIDE), 1)
    rows = pl.ds(pl.multiple_of(chunk * ROWS, ROWS), ROWS)
    picked = jnp.zeros((ROWS, SIDE), F32)
    for b in range(BLOCKS):
        column = lane + b * SIDE
        inside = (column >= start) & (column < start + SIDE)
        picked = jnp.where(inside, obj[part, rows, b * SIDE:(b + 1) * SIDE], picked)
    return picked


def row_index(chunk):
    return lax.broadcasted_iota(jnp.int32, (ROWS, SIDE), 0) + chunk * ROWS


def wave_kernel(
    n_tile,
    obj_in, probe_in, chirp_in, amp_in, srow_in, scol_in, count, tab_in,
    out,
    obj, probe, chirp, amp, srow, scol, tab,
    pos, send_a, recv_a, send_b, recv_b, asm, win, grad, got, total,
    first, second, psi, vert, residual,
    in_sem, obj_sem, pos_sem, amp_sem, a_sem, b_sem, xs_sem, xr_sem, gs_sem, gr_sem, fs_sem, fr_sem,
    out_sem,
):
    k = lax.axis_index("cuts")
    t = lax.axis_index("tile")
    core = lax.rem(t, 2)
    following = lax.rem(t + 1, n_tile)
    previous = lax.rem(t + n_tile - 1, n_tile)
    alpha = k // 2
    computing = lax.rem(k, 2) == core

    def target(which):
        return 2 * which + core

    ints = [
        pltpu.make_async_copy(srow_in, srow, in_sem.at[0]),
        pltpu.make_async_copy(scol_in, scol, in_sem.at[1]),
    ]
    tables = [
        pltpu.make_async_copy(chirp_in, chirp, in_sem.at[3]),
        pltpu.make_async_copy(tab_in, tab, in_sem.at[4]),
        pltpu.make_async_copy(probe_in, probe, in_sem.at[5]),
        pltpu.make_async_copy(amp_in.at[0], amp.at[0], in_sem.at[6]),
    ]

    def load(c):
        rows = pl.ds(pl.multiple_of(c * ROWS, ROWS), ROWS)
        return pltpu.make_async_copy(obj_in.at[0, :, rows], obj.at[:, rows], obj_sem.at[c])

    barrier = pltpu.get_barrier_semaphore()
    for step in range(1, 4):
        pl.semaphore_signal(
            barrier, inc=1, device_id=(lax.rem(k + step, 4), t), device_id_type=MESH
        )
    for neighbour in (following, previous):
        pl.semaphore_signal(barrier, inc=1, device_id=(k, neighbour), device_id_type=MESH)

    for copy in ints:
        copy.start()
    each(CHUNKS, lambda c: load(c).start())

    @pl.when(computing)
    def _():
        for copy in tables:
            copy.start()

    for copy in ints:
        copy.wait()
    line = lax.broadcasted_iota(jnp.int32, (8, 128), 0)
    mine = jnp.zeros((8, 128), jnp.int32)
    for i, value in enumerate((srow[0], srow[1], scol[0], scol[1], count[0])):
        mine = jnp.where(line == i, value, mine)
    pos[0] = mine
    pl.semaphore_wait(barrier, 5)

    def remote(source, sink, send, recv, device):
        return pltpu.make_async_remote_copy(
            src_ref=source, dst_ref=sink, send_sem=send, recv_sem=recv,
            device_id=device, device_id_type=MESH,
        )

    pos_copy = remote(pos.at[0], pos.at[1], pos_sem.at[0], pos_sem.at[1], (k, following))
    pos_copy.start()

    def a_copy(c):
        return remote(send_a.at[c], recv_a.at[c], a_sem.at[0, c], a_sem.at[1, c], (k, following))

    def b_copy(c):
        return remote(send_b.at[c], recv_b.at[c], b_sem.at[0, c], b_sem.at[1, c], (k, previous))

    start_a = wide(pos[0, 3:4, :])

    def begin_a(c):
        load(c).wait()
        for part in range(2):
            send_a[c, part] = column_select(obj, part, c, start_a).astype(BF)
        a_copy(c).start()

    each(CHUNKS, begin_a)

    amp_copy = remote(amp_in.at[1], amp.at[1], amp_sem.at[0], amp_sem.at[1], (k, following))
    sends_amp = (alpha == 1) & (lax.rem(k, 2) == lax.rem(following, 2))
    takes_amp = (alpha == 1) & computing

    @pl.when(sends_amp)
    def _():
        amp_copy.start()

    @pl.when(computing)
    def _():
        for copy in tables:
            copy.wait()
        t_r, t_i = tab[0].astype(BF), tab[1].astype(BF)
        first[1] = block(t_r, t_i)
        second[1] = block_t(t_r, t_i)
        angle = chirp[...]
        turn_r, turn_i = jnp.cos(angle), jnp.sin(angle)
        s_r = tab[0] * turn_r + tab[1] * turn_i
        s_i = tab[0] * turn_i - tab[1] * turn_r
        scaled = jnp.concatenate([s_r, s_i], axis=1)
        big = scaled.astype(BF)
        small = (scaled - big.astype(F32)).astype(BF)
        f_high = second[1]
        f_low = block_t((tab[0] - t_r.astype(F32)).astype(BF), (tab[1] - t_i.astype(F32)).astype(BF))
        prop = mm(big, f_high) + (mm(big, f_low) + mm(small, f_high))
        p_r, p_i = prop[:, :SIDE], prop[:, SIDE:]
        first[0] = block(p_r.astype(BF), p_i.astype(BF))
        second[0] = block_t(p_r.T.astype(BF), p_i.T.astype(BF))

    pos_copy.wait_recv()
    start_b = wide(pos[1, 2:3, :])

    def begin_b(c):
        for part in range(2):
            send_b[c, part] = column_select(obj, part, c, start_b).astype(BF)
        b_copy(c).start()

    each(CHUNKS, begin_b)

    @pl.when(computing)
    def _():
        first_slot = alpha == 0
        row_start = wide(jnp.where(first_slot, pos[0, 0:1, :], pos[1, 1:2, :]))
        col_start = wide(jnp.where(first_slot, pos[0, 2:3, :], pos[1, 3:4, :]))
        down = lax.broadcasted_iota(jnp.int32, (SIDE, SIDE), 0)
        across = lax.broadcasted_iota(jnp.int32, (SIDE, SIDE), 1)
        row_turn = jnp.where(((down - across - row_start) & (SIDE - 1)) == 0, 1.0, 0.0).astype(BF)
        col_turn = jnp.where(((across - down - col_start) & (SIDE - 1)) == 0, 1.0, 0.0).astype(BF)
        for part in range(2):
            half = mm(row_turn, probe[part]).astype(BF)
            psi[0, :, part * SIDE:(part + 1) * SIDE] = mm(half, col_turn)

    def send_window(which, c):
        return remote(
            asm.at[which, c], win.at[k, c], xs_sem.at[which, c], xr_sem.at[k, c],
            (target(which), t),
        )

    edge = [wide(pos[0, 0:1, :]), wide(pos[1, 1:2, :])]
    left = [wide(pos[0, 2:3, :]), wide(pos[1, 3:4, :])]

    def put_together(which, c):
        own = [column_select(obj, part, c, left[which]) for part in range(2)]
        upper = row_index(c) >= edge[which]
        if which == 1:
            a_copy(c).wait_recv()
        else:
            b_copy(c).wait_recv()
        for part in range(2):
            if which == 1:
                piece = jnp.where(upper, recv_a[c, part].astype(F32), own[part])
            else:
                piece = jnp.where(upper, own[part], recv_b[c, part].astype(F32))
            asm[which, c, part] = piece.astype(BF)

        @pl.when(k != target(which))
        def _():
            send_window(which, c).start()

        @pl.when(k == target(which))
        def _():
            win[k, c] = asm[which, c]

    def near_first(action):
        for side, order in ((0, (0, 1)), (1, (1, 0))):
            @pl.when(core == side)
            def _():
                for which in order:
                    each(CHUNKS, functools.partial(action, which))

    near_first(put_together)

    def give_back(layer, c):
        return remote(
            grad.at[layer, c], got.at[alpha, c], gs_sem.at[layer, c], gr_sem.at[alpha, c],
            (layer, t),
        )

    @pl.when(computing)
    def _():
        def window(layer):
            return [win[layer, :, part].reshape(SIDE, SIDE).astype(F32) for part in range(2)]

        def ahead(layer):
            @pl.when(k != layer)
            def _():
                each(CHUNKS, lambda c: remote(
                    win.at[layer, c], win.at[layer, c], xs_sem.at[0, c], xr_sem.at[layer, c], (layer, t)
                ).wait_recv())

            far = layer // 3
            w_r, w_i = window(layer)
            s_r, s_i = psi[layer, :, :SIDE], psi[layer, :, SIDE:]
            vert[:SIDE] = (s_r * w_r - s_i * w_i).astype(BF)
            vert[SIDE:] = (s_r * w_i + s_i * w_r).astype(BF)
            for part in range(2):
                side = slice(part * SIDE, (part + 1) * SIDE)
                residual[:, side] = mm(first[far, side], vert[...]).astype(BF)
            for part in range(2):
                side = slice(part * SIDE, (part + 1) * SIDE)
                psi[layer + 1, :, side] = mm(residual[...], second[far, :, side])

        each(4, ahead)

        e_r, e_i = psi[4, :, :SIDE], psi[4, :, SIDE:]

        @pl.when(takes_amp)
        def _():
            amp_copy.wait_recv()

        live = wide(
            jnp.where(
                alpha == 0, jnp.where(pos[0, 4:5, :] > 0, 1.0, 0.0), jnp.where(pos[1, 4:5, :] > 1, 1.0, 0.0)
            )
        )
        measured = amp[alpha].astype(F32)
        factor = live * (1.0 - measured * lax.rsqrt(e_r * e_r + e_i * e_i + 0.01))
        residual[:, :SIDE] = (factor * e_r).astype(BF)
        residual[:, SIDE:] = (factor * e_i).astype(BF)

        def behind(step):
            layer = 3 - step
            far = layer // 3
            for part in range(2):
                side = slice(part * SIDE, (part + 1) * SIDE)
                vert[side] = mm(residual[...], first[far, :, side]).astype(BF)
            h_r, h_i = mm(second[far, :SIDE], vert[...]), mm(second[far, SIDE:], vert[...])
            s_r, s_i = psi[layer, :, :SIDE], psi[layer, :, SIDE:]
            w_r, w_i = window(layer)
            grad[layer, :, 0] = (h_r * s_r + h_i * s_i).astype(BF).reshape(CHUNKS, ROWS, SIDE)
            grad[layer, :, 1] = (h_i * s_r - h_r * s_i).astype(BF).reshape(CHUNKS, ROWS, SIDE)
            residual[:, :SIDE] = (h_r * w_r + h_i * w_i).astype(BF)
            residual[:, SIDE:] = (h_i * w_r - h_r * w_i).astype(BF)

            @pl.when(k != layer)
            def _():
                each(CHUNKS, lambda c: give_back(layer, c).start())

            @pl.when(k == layer)
            def _():
                got[alpha] = grad[layer]

        each(4, behind)

    def forward(which, c):
        return remote(
            got.at[which, c], got.at[2 + which, c], fs_sem.at[which, c], fr_sem.at[which, c],
            (k, following if which == 0 else previous),
        )

    def collect(which, c):
        @pl.when(k != target(which))
        def _():
            remote(
                grad.at[0, c], got.at[which, c], gs_sem.at[0, c], gr_sem.at[which, c], (target(which), t)
            ).wait_recv()

        forward(which, c).start()

    near_first(collect)

    def give_out(c):
        rows = pl.ds(pl.multiple_of(c * ROWS, ROWS), ROWS)
        return pltpu.make_async_copy(total.at[:, rows], out.at[0, :, rows], out_sem.at[c])

    edges = [edge[0], edge[1], wide(pos[1, 0:1, :]), wide(pos[0, 1:2, :])]
    lefts = [left[0], left[1], wide(pos[1, 2:3, :]), wide(pos[0, 3:4, :])]
    lane = lax.broadcasted_iota(jnp.int32, (1, SIDE), 1)

    def add_up(c):
        rows = pl.ds(pl.multiple_of(c * ROWS, ROWS), ROWS)
        row = row_index(c)
        for which in range(2):
            forward(which, c).wait_recv()
        for part in range(2):
            pieces = []
            for s in range(4):
                held = row >= edges[s] if s in (0, 3) else row < edges[s]
                pieces.append(jnp.where(held, got[s, c, part].astype(F32), 0.0))
            for b in range(BLOCKS):
                column = lane + b * SIDE
                sums = jnp.zeros((ROWS, SIDE), F32)
                for s in range(4):
                    inside = (column >= lefts[s]) & (column < lefts[s] + SIDE)
                    sums = sums + jnp.where(inside, pieces[s], 0.0)
                total[part, rows, b * SIDE:(b + 1) * SIDE] = sums
        give_out(c).start()

    each(CHUNKS, add_up)

    pos_copy.wait_send()

    @pl.when(sends_amp)
    def _():
        amp_copy.wait_send()

    def finish(c):
        a_copy(c).wait_send()
        b_copy(c).wait_send()
        for which in range(2):
            @pl.when(k != target(which))
            def _():
                send_window(which, c).wait_send()

    each(CHUNKS, finish)

    @pl.when(computing)
    def _():
        def given(layer):
            @pl.when(k != layer)
            def _():
                each(CHUNKS, lambda c: give_back(layer, c).wait_send())

        each(4, given)

    def leave(c):
        for which in range(2):
            forward(which, c).wait_send()
        give_out(c).wait()

    each(CHUNKS, leave)


def body(object_field, probe_wave, chirp_phase, amplitude, scan_row, scan_col, view_count):
    n_tile = lax.axis_size("tile")
    anywhere = pl.BlockSpec(memory_space=pl.ANY)
    dma = pltpu.SemaphoreType.DMA
    return pl.pallas_call(
        functools.partial(wave_kernel, n_tile),
        out_shape=pltpu.VMEM((1, 2, SIDE, BLOCKS * SIDE), F32),
        in_specs=[anywhere] * 6 + [pl.BlockSpec(memory_space=pltpu.SMEM), anywhere],
        out_specs=anywhere,
        scratch_shapes=[
            pltpu.VMEM((2, SIDE, BLOCKS * SIDE), F32),
            pltpu.VMEM((2, SIDE, SIDE), BF),
            pltpu.VMEM((1, SIDE), F32),
            pltpu.VMEM((2, SIDE, SIDE), BF),
            pltpu.SMEM((2,), jnp.int32),
            pltpu.SMEM((2,), jnp.int32),
            pltpu.VMEM((2, SIDE, SIDE), F32),
            pltpu.VMEM((2, 8, 128), jnp.int32),
            pltpu.VMEM((CHUNKS, 2, ROWS, SIDE), BF),
            pltpu.VMEM((CHUNKS, 2, ROWS, SIDE), BF),
            pltpu.VMEM((CHUNKS, 2, ROWS, SIDE), BF),
            pltpu.VMEM((CHUNKS, 2, ROWS, SIDE), BF),
            pltpu.VMEM((2, CHUNKS, 2, ROWS, SIDE), BF),
            pltpu.VMEM((4, CHUNKS, 2, ROWS, SIDE), BF),
            pltpu.VMEM((4, CHUNKS, 2, ROWS, SIDE), BF),
            pltpu.VMEM((4, CHUNKS, 2, ROWS, SIDE), BF),
            pltpu.VMEM((2, SIDE, BLOCKS * SIDE), F32),
            pltpu.VMEM((2, 2 * SIDE, 2 * SIDE), BF),
            pltpu.VMEM((2, 2 * SIDE, 2 * SIDE), BF),
            pltpu.VMEM((5, SIDE, 2 * SIDE), F32),
            pltpu.VMEM((2 * SIDE, SIDE), BF),
            pltpu.VMEM((SIDE, 2 * SIDE), BF),
            dma((7,)),
            dma((CHUNKS,)),
            dma((2,)),
            dma((2,)),
            dma((2, CHUNKS)),
            dma((2, CHUNKS)),
            dma((2, CHUNKS)),
            dma((4, CHUNKS)),
            dma((4, CHUNKS)),
            dma((2, CHUNKS)),
            dma((2, CHUNKS)),
            dma((2, CHUNKS)),
            dma((CHUNKS,)),
        ],
        compiler_params=pltpu.CompilerParams(
            collective_id=0, has_side_effects=True, vmem_limit_bytes=48 * 1024 * 1024
        ),
        name="waves",
    )(
        *(
            value if value.size == 1 else pltpu.with_memory_space_constraint(value, pltpu.HBM)
            for value in (
                object_field, probe_wave, chirp_phase.reshape(1, SIDE), amplitude,
                scan_row, scan_col, view_count, jnp.asarray(fourier_constants()),
            )
        )
    )


def solution(mesh):
    in_specs = (
        P("cuts", None, "tile", None),
        P(),
        P(),
        P("tile", None, None),
        P("tile"),
        P("tile"),
        P("tile"),
    )
    return jax.shard_map(
        body, mesh=mesh, in_specs=in_specs, out_specs=P("cuts", None, "tile", None), check_vma=False
    )
```
